512 devices in a mesh: dp: 64 (over z, x_hi, core), head: 8 (over y, x_lo).
Axes of the slice: x: 4 (x_hi: 2, x_lo: 2; x = x_hi * 2 + x_lo), y: 4, z: 16, core: 2. Of those that a mesh axis runs over, the one named last changes fastest.
Arguments:
- query_clean: float32 [16384, 8192], P(('dp', 'head')), may hold values from -320 to 320
- key_clean: float32 [16384, 1024], P(('dp', 'head')), may hold values from -12 to 12
- clean_value_rows: float32 [16384, 1024], P(('dp', 'head')), may hold values from -6 to 6
- query_corrupt: float32 [16384, 8192], P(('dp', 'head')), may hold values from -320 to 320
- key_corrupt: float32 [16384, 1024], P(('dp', 'head')), may hold values from -12 to 12
- corrupted_value_rows: float32 [16384, 1024], P(('dp', 'head')), may hold values from -6 to 6
- cotangent: float32 [16384, 8192], P(('dp', 'head')), may hold values from -0.3 to 0.3
- bin_segments: int32 [64, 256], P('dp'), may hold values from 0 to 3, never falling along the last dimension, each value on 1 to 128 neighbouring positions
- plan: int32 [64, 64], P('dp'), may hold values from 0 to 63, each once within a row
- offsets: int32 [64], replicated, may hold values from 0 to 63, each once
Outputs:
- head_scores: float32 [256, 64], P('dp', 'head')
- query_scores: float32 [256, 64], P('dp', 'head')
- kv_scores: float32 [256, 8], P('dp', 'head')
The draws below stay inside these ranges and needn't reach their ends.
Inputs may be any that keep to these rules, and one draw needn't show every extreme that they name: `plan`: each row is a permutation of 0 to 63. `offsets`: a permutation: every bin receives exactly one block from each dp index.
All inputs are finite; a program needn't handle non-finite values.
Results may differ from the reference program's by a relative error of at most 0.0003.
Values sent between devices are 32-bit elements; how exact they have to be, the bound alone decides.
A program may use at most 64 MiB of HBM per device.

```python
import math
import jax
import jax.numpy as jnp
import numpy as np
from jax import lax

QUERY_HEADS = 64
KEY_VALUE_HEADS = 8
HEAD_SIZE = 128
PACK = 256
PAIRS_PER_BIN = 4
NBLK = 64
TOKEN_ROWS_ALL = 16384
N_DP = 64


def query_key(key, salt):
    basis = jax.random.fold_in(key, salt)
    query_random_seed, key_random_seed = jax.random.split(basis, 2)
    key_collections = jnp.clip(jax.random.normal(key_random_seed, (TOKEN_ROWS_ALL, KEY_VALUE_HEADS, HEAD_SIZE), jnp.float32), -6.0, 6.0)
    query_matrix = jnp.clip(jax.random.normal(query_random_seed, (TOKEN_ROWS_ALL, KEY_VALUE_HEADS, QUERY_HEADS // KEY_VALUE_HEADS, HEAD_SIZE), jnp.float32), -6.0, 6.0)
    return (query_matrix.reshape(TOKEN_ROWS_ALL, QUERY_HEADS * HEAD_SIZE), key_collections.reshape(TOKEN_ROWS_ALL, KEY_VALUE_HEADS * HEAD_SIZE))


def draw_query_clean(key, part):
    return query_key(key, 11)[0]


def draw_key_clean(key, part):
    return query_key(key, 11)[1]


def draw_query_corrupt(key, part):
    return query_key(key, 23)[0]


def draw_key_corrupt(key, part):
    return query_key(key, 23)[1]


def block_scale(own_key, shape, cuts, least, largest):
    def one(position, shards_of):
        heights = jax.random.uniform(jax.random.fold_in(jax.random.fold_in(own_key, 6), position), (shards_of,), jnp.float32, least / len(cuts), largest / len(cuts))
        return jnp.repeat(jnp.exp(heights), shape[position] // shards_of).reshape((-1,) + (1,) * (len(shape) - position - 1))

    level = one(*cuts[0])
    for cut in cuts[1:]:
        level = level * one(*cut)
    return level


def profile(number_of, total, limit, slope):
    weights = [(1 << 20) // math.isqrt(standing ** slope) + 1 for standing in range(2, number_of + 1)]
    spare, holding = total - limit - (number_of - 1), [1] * (number_of - 1)
    while spare > 0:
        movable = [i for i in range(number_of - 1) if holding[i] < limit]
        mass, budget = sum([weights[i] for i in movable]), spare
        for i in movable:
            more = min(limit - holding[i], max(1, budget * weights[i] // mass), spare)
            holding[i] = holding[i] + more
            spare = spare - more
    return np.array([limit] + holding)


def ragged(own_key, number_of, total, most, skew):
    if number_of == 2:
        one = jax.random.randint(own_key, (), max(1, total - most), min(most, total - 1) + 1)
        return jnp.stack([one, total - one])
    lengths = jnp.asarray(profile(number_of, total, most, skew), jnp.int32)
    twos = (number_of - 1) // 2
    giver, taker = lengths[1:1 + 2 * twos:2], lengths[2:2 + 2 * twos:2]
    slack = jnp.minimum(giver - 1, most - taker)
    moved = jax.random.randint(jax.random.fold_in(own_key, 1), (twos,), 0, 1 << 20) % (slack + 1)
    lengths = lengths.at[1:1 + 2 * twos:2].set(giver - moved).at[2:2 + 2 * twos:2].set(taker + moved)
    return lengths[jax.random.permutation(jax.random.fold_in(own_key, 2), number_of)]


def gaussian(own_key, shape, scale, most, pieces=(), kind=jnp.bfloat16):
    entries = scale * jax.random.normal(own_key, shape, jnp.float32)
    if pieces:
        entries = entries * block_scale(own_key, shape, pieces, -0.22, 0.18)
    return jnp.clip(entries, -most, most).astype(kind)


def setup_inputs(seed: int = 0) -> dict:
    keys = jax.random.split(jax.random.key(seed), 11)
    query_clean = draw_query_clean(jax.random.fold_in(keys[10], 71), 0)
    key_clean = draw_key_clean(jax.random.fold_in(keys[10], 71), 0)
    clean_value_rows = gaussian(keys[2], (TOKEN_ROWS_ALL, KEY_VALUE_HEADS * HEAD_SIZE), 1.0, 6.0, ((0, 512),), jnp.float32)
    query_corrupt = draw_query_corrupt(jax.random.fold_in(keys[10], 71), 0)
    key_corrupt = draw_key_corrupt(jax.random.fold_in(keys[10], 71), 0)
    corrupted_value_rows = gaussian(keys[5], (TOKEN_ROWS_ALL, KEY_VALUE_HEADS * HEAD_SIZE), 1.0, 6.0, ((0, 512),), jnp.float32)
    cotangent = gaussian(keys[6], (TOKEN_ROWS_ALL, QUERY_HEADS * HEAD_SIZE), 0.05, 0.3, ((0, 512),), jnp.float32)
    bin_segments = jax.vmap(lambda own: jnp.searchsorted(jnp.cumsum(ragged(own, PAIRS_PER_BIN, PACK, PACK // 2, 2)), jnp.arange(PACK), side="right"))(jax.random.split(keys[7], N_DP)).reshape((N_DP, PACK)).astype(jnp.int32)
    plan = jax.vmap(lambda own: jax.random.permutation(own, NBLK))(jax.random.split(keys[8], N_DP)).reshape((N_DP, NBLK)).astype(jnp.int32)
    offsets = jax.random.permutation(keys[9], NBLK).astype(jnp.int32)
    return dict(query_clean=query_clean, key_clean=key_clean, clean_value_rows=clean_value_rows, query_corrupt=query_corrupt, key_corrupt=key_corrupt, corrupted_value_rows=corrupted_value_rows, cotangent=cotangent, bin_segments=bin_segments, plan=plan, offsets=offsets)


TOP_PRECISION = lax.Precision.HIGHEST


def as_views(query_rows, key_rows, value_rows):
    rows_here = query_rows.shape[0]
    width = key_rows.shape[1] // HEAD_SIZE
    groups = query_rows.shape[1] // key_rows.shape[1]
    return (query_rows.reshape(rows_here, width, groups, HEAD_SIZE), key_rows.reshape(rows_here, width, HEAD_SIZE), value_rows.reshape(rows_here, width, HEAD_SIZE))


def attend(query_matrix, key_collections, value_collection, allowed):
    scale_factor = query_matrix.shape[-1] ** -0.5
    score_matrix = jnp.einsum("thxn,whn->hxtw", query_matrix, key_collections, precision=TOP_PRECISION) * scale_factor
    score_matrix = jnp.where(allowed, score_matrix, -jnp.inf)
    peak = jnp.max(score_matrix, axis=-1, keepdims=True)
    raised = jnp.exp(score_matrix - peak)
    weight_matrix = raised / jnp.sum(raised, axis=-1, keepdims=True)
    output_tensors = jnp.einsum("whfo,owj->fwhj", weight_matrix, value_collection, precision=TOP_PRECISION)
    return weight_matrix, output_tensors


def attribute(clean_views, clean_pass, corrupt_views, cotangent, allowed):
    query_matrix, key_collections, value_collection = clean_views
    weight_matrix, output_tensors = clean_pass
    query_other, key_other, value_other = corrupt_views
    scale_factor = query_matrix.shape[-1] ** -0.5
    other_outputs = attend(query_other, key_other, value_other, allowed)[1]
    value_gradient = jnp.einsum("xprv,rxpw->vxw", weight_matrix, cotangent, precision=TOP_PRECISION)
    weight_gradient = jnp.einsum("thxn,whn->hxtw", cotangent, value_collection, precision=TOP_PRECISION)
    row_dot = jnp.transpose(jnp.sum(cotangent * output_tensors, axis=-1), (1, 2, 0))[..., None]
    score_gradient = weight_matrix * (weight_gradient - row_dot) * scale_factor
    query_gradient = jnp.einsum("whfo,owj->fwhj", score_gradient, key_collections, precision=TOP_PRECISION)
    key_gradient = jnp.einsum("xprv,rxpw->vxw", score_gradient, query_matrix, precision=TOP_PRECISION)
    head_terms = jnp.sum((other_outputs - output_tensors) * cotangent, axis=-1)
    query_terms = jnp.sum((query_other - query_matrix) * query_gradient, axis=-1)
    kv_terms = jnp.sum((key_other - key_collections) * key_gradient + (value_other - value_collection) * value_gradient, axis=-1)
    rows_here = query_matrix.shape[0]
    return head_terms.reshape(rows_here, -1), query_terms.reshape(rows_here, -1), kv_terms


def causal_mask(segment_ids):
    row_index = jnp.arange(segment_ids.shape[0], dtype=jnp.int32)
    same = segment_ids[:, None] == segment_ids[None, :]
    return jnp.logical_and(same, row_index[:, None] >= row_index[None, :])


def pair_sums(segment_ids, term_sets):
    members = (segment_ids[:, None] == jnp.arange(PAIRS_PER_BIN, dtype=jnp.int32)[None, :]).astype(jnp.float32)
    return tuple(jnp.dot(members.T, column_set, precision=TOP_PRECISION) for column_set in term_sets)


def reference(query_clean, key_clean, clean_value_rows, query_corrupt, key_corrupt, corrupted_value_rows, cotangent, bin_segments, plan, offsets):
    block_count = offsets.shape[0]
    block_rows = PACK // block_count
    inverse = jnp.zeros((N_DP, block_count), jnp.int32).at[jnp.arange(N_DP, dtype=jnp.int32)[:, None], plan].set(
        jnp.broadcast_to(jnp.arange(block_count, dtype=jnp.int32)[None, :], (N_DP, block_count)))
    arrays = (query_clean, key_clean, clean_value_rows, query_corrupt, key_corrupt, corrupted_value_rows, cotangent)

    def one_bin(bin_index):
        sources = ((bin_index - offsets) % N_DP).astype(jnp.int32)
        which = inverse[sources, jnp.arange(block_count, dtype=jnp.int32)]

        def collect(source_array):
            blocks = source_array.reshape(N_DP, block_count, block_rows, source_array.shape[1])
            return blocks[sources, which].reshape(PACK, source_array.shape[1])

        packed = [collect(source_array) for source_array in arrays]
        segment_ids = bin_segments[bin_index]
        allowed = causal_mask(segment_ids)
        clean_views = as_views(packed[0], packed[1], packed[2])
        corrupt_views = as_views(packed[3], packed[4], packed[5])
        cot_view = packed[6].reshape(clean_views[0].shape)
        clean_pass = attend(clean_views[0], clean_views[1], clean_views[2], allowed)
        term_sets = attribute(clean_views, clean_pass, corrupt_views, cot_view, allowed)
        return pair_sums(segment_ids, term_sets)

    head_portion, query_portion, key_value_portion = lax.map(one_bin, jnp.arange(N_DP, dtype=jnp.int32))
    return (head_portion.reshape(N_DP * PAIRS_PER_BIN, QUERY_HEADS), query_portion.reshape(N_DP * PAIRS_PER_BIN, QUERY_HEADS), key_value_portion.reshape(N_DP * PAIRS_PER_BIN, KEY_VALUE_HEADS))
```

```python
import functools

import jax
import jax.numpy as jnp
from jax import lax
from jax.experimental import pallas as pl
from jax.experimental.pallas import tpu as pltpu
from jax.sharding import PartitionSpec as P

MESH = pl.DeviceIdType.MESH
F32 = jnp.float32
BF16 = jnp.bfloat16
HEAD_SIZE = 128
PAIRS_PER_BIN = 4
ROWS = 4
SUB = 4
CHUNKS = 4


def iota(shape, dim):
    return lax.broadcasted_iota(jnp.int32, shape, dim)


def split3(x):
    high = x.astype(BF16)
    rest = x - high.astype(F32)
    middle = rest.astype(BF16)
    low = (rest - middle.astype(F32)).astype(BF16)
    return high, middle, low


def left_terms(x):
    high, middle, low = split3(x)
    return jnp.concatenate([high, middle, high, middle, high, low], axis=1)


def right_terms(x):
    high, middle, low = split3(x)
    return jnp.concatenate([high, middle, middle, high, low, high], axis=1)


def product(left, right):
    return lax.dot_general(left, right, (((1,), (1,)), ((), ())), preferred_element_type=F32)


def kernel(
    n, heads, group,
    query, key, value, query_other, key_other, value_other, cotangent, segments, plan, offsets,
    head_out, query_out, kv_out,
    first_kv, first_q, send_kv, send_q, bin_kv, bin_q,
    key_terms, value_terms, bias, sums, loose, segments_other, part_out, part_in,
    send1, recv1, send2, recv2, small_send, small_recv,
):
    me = lax.axis_index("dp")
    head = lax.axis_index("head")
    half = n // 2
    ring = n // SUB
    width = HEAD_SIZE
    rows_here = ROWS * n // heads
    per_chunk = group // CHUNKS
    chunk_width = per_chunk * width
    z, sub = me // SUB, me % SUB
    odd_core = sub % 2
    pair = me % half
    own_bit = me // half
    partner = (me + half) % n

    barrier = pltpu.get_barrier_semaphore()

    def greet_dp(i, carry):
        pl.semaphore_signal(barrier, inc=1, device_id=((me + i) % n, head), device_id_type=MESH)
        return carry

    def greet_head(i, carry):
        pl.semaphore_signal(barrier, inc=1, device_id=(me, (head + i) % heads), device_id_type=MESH)
        return carry

    lax.fori_loop(1, heads, greet_head, 0)
    lax.fori_loop(1, n, greet_dp, 0)
    pl.semaphore_wait(barrier, n - 1 + heads - 1)

    def sources(chunk, j):
        if chunk == 0:
            for place, ref in enumerate((key, value, key_other, value_other)):
                yield ref, pl.multiple_of(j * width, width), width, place * width
        else:
            begin = (chunk - 1) * chunk_width
            for place, ref in enumerate((query, query_other, cotangent)):
                at = pl.multiple_of(j * (group * width) + begin, width)
                yield ref, at, chunk_width, place * chunk_width

    def first_of(chunk):
        return first_kv if chunk == 0 else first_q.at[chunk - 1]

    def send_of(chunk):
        return send_kv if chunk == 0 else send_q.at[chunk - 1]

    def bin_of(chunk):
        return bin_kv if chunk == 0 else bin_q.at[chunk - 1]

    def start_first(chunk):
        at = pl.multiple_of(head * rows_here, 8)

        def to(i, carry):
            j = (head + i) % heads
            for ref, column, columns, place in sources(chunk, j):
                pltpu.make_async_remote_copy(
                    src_ref=ref.at[:, pl.ds(column, columns)],
                    dst_ref=first_of(chunk).at[pl.ds(at, rows_here), pl.ds(place, columns)],
                    send_sem=send1.at[chunk],
                    recv_sem=recv1.at[chunk],
                    device_id=(me, j),
                    device_id_type=MESH,
                ).start()
            return carry

        lax.fori_loop(1, heads, to, 0)
        for ref, column, columns, place in sources(chunk, head):
            pltpu.make_async_copy(
                ref.at[:, pl.ds(column, columns)],
                first_of(chunk).at[pl.ds(at, rows_here), pl.ds(place, columns)],
                recv1.at[chunk],
            ).start()

    def wait_for(ref, semaphore):
        pltpu.make_async_copy(ref, ref, semaphore).wait()

    def step_along(j, count, flipped):
        size = (count - j) // 2
        sign = (1 - 2 * (j % 2)) * (1 - 2 * flipped)
        return sign * size

    def start_second(chunk):
        count = ring if chunk == 0 else ring // 2

        def copy(t, remote):
            j, i = t // SUB, t % SUB
            z_to = (z + step_along(j, count, odd_core) + ring) % ring
            to = z_to * SUB + (sub + 1 + i) % SUB
            slot = me if chunk == 0 else j * SUB + sub
            source = send_of(chunk).at[pl.ds(pl.multiple_of(to % half * 8, 8), 8)]
            target = bin_of(chunk).at[pl.ds(pl.multiple_of(slot * 8, 8), 8)]
            if not remote:
                pltpu.make_async_copy(source, target, recv2.at[chunk]).start()
                return
            pltpu.make_async_remote_copy(
                src_ref=source,
                dst_ref=target,
                send_sem=send2.at[chunk],
                recv_sem=recv2.at[chunk],
                device_id=(to, head),
                device_id_type=MESH,
            ).start()

        def step(t, carry):
            copy(t, True)
            return carry

        last = count * SUB - 1
        lax.fori_loop(0, last, step, 0)
        copy(last, False)

    start_first(0)
    start_first(1)
    segment_copy = pltpu.make_async_remote_copy(
        src_ref=segments,
        dst_ref=segments_other,
        send_sem=small_send.at[0],
        recv_sem=small_recv.at[0],
        device_id=(partner, head),
        device_id_type=MESH,
    )
    segment_copy.start()

    off_row = offsets[...].astype(F32)
    plan_row = plan[...].astype(F32)
    square = (n, n)
    same = iota(square, 0) == iota(square, 1)
    lanes = iota(square, 1).astype(F32)
    off_column = jnp.sum(jnp.where(same, off_row, 0.0), axis=1, keepdims=True)
    plan_column = jnp.sum(jnp.where(same, plan_row, 0.0), axis=1, keepdims=True)
    distance = jnp.sum(jnp.where(plan_column == lanes, off_row, 0.0), axis=1, keepdims=True)
    target = me.astype(F32) + distance
    target = jnp.where(target >= n, target - n, target)
    wide = (n, ROWS * n)
    block = iota(wide, 1) // ROWS
    target_row = jnp.sum(jnp.where(iota(wide, 0) == block, target, 0.0), axis=0, keepdims=True)
    one = (1, ROWS * n)
    key_in = target_row * ROWS + (iota(one, 1) % ROWS).astype(F32)
    out = iota((ROWS * n, 1), 0)
    key_to = ((out // 8 + half * (out % 2)) * ROWS + out % 8 // 2).astype(F32)
    order = jnp.where(key_to == key_in, 1.0, 0.0).astype(BF16)

    def reorder(chunk):
        source, place = first_of(chunk), send_of(chunk)
        columns = 4 * width if chunk == 0 else 3 * chunk_width
        for begin in range(0, columns, 256):
            high, middle, low = split3(source[:, begin : begin + 256])
            moved = jnp.dot(order, high, preferred_element_type=F32)
            moved += jnp.dot(order, middle, preferred_element_type=F32)
            moved += jnp.dot(order, low, preferred_element_type=F32)
            place[:, begin : begin + 256] = moved

    for chunk in range(CHUNKS + 1):
        wait_for(first_of(chunk), recv1.at[chunk])
        reorder(chunk)
        start_second(chunk)
        if chunk + 2 <= CHUNKS:
            start_first(chunk + 2)

    segment_copy.wait()
    q_index = iota((half * ROWS, 1), 0)
    slot = q_index // ROWS
    slot_sub = slot % SUB
    slot_z = z - step_along(slot // SUB, ring // 2, slot_sub % 2)
    q_source = (slot_z + ring) % ring * SUB + slot_sub
    k_source = iota(one, 1) // ROWS
    members = []
    for bit in range(2):
        which = pair + bit * half
        segment = jnp.where(own_bit == bit, segments[...], segments_other[...])
        starts = [
            jnp.sum(jnp.where(segment < g, 1.0, 0.0), axis=1, keepdims=True)
            for g in range(1, PAIRS_PER_BIN)
        ]
        k_distance = ((which - k_source + n) % n).astype(F32)
        k_slot = jnp.sum(
            jnp.where(off_column == k_distance, iota(wide, 0).astype(F32), 0.0), axis=0, keepdims=True
        )
        k_place = k_slot * ROWS + (iota(one, 1) % ROWS).astype(F32)
        q_distance = ((which - q_source + n) % n).astype(F32)
        tall = (half * ROWS, n)
        q_slot = jnp.sum(
            jnp.where(off_row == q_distance, iota(tall, 1).astype(F32), 0.0), axis=1, keepdims=True
        )
        q_place = q_slot * ROWS + (q_index % ROWS).astype(F32)
        begin = jnp.zeros_like(q_place)
        k_segment = jnp.zeros_like(k_place)
        for start in starts:
            begin = jnp.where(q_place >= start, start, begin)
            k_segment += jnp.where(k_place >= start, 1.0, 0.0)
        allowed = jnp.logical_and(k_place <= q_place, k_place >= begin)
        bias[bit] = jnp.where(allowed, 0.0, -jnp.inf)
        members.append(
            jnp.where(k_segment == iota((8, ROWS * n), 0).astype(F32), 1.0, 0.0)
        )

    wait_for(bin_kv, recv2.at[0])
    keys = ROWS * n
    for place, (terms, begin) in enumerate(
        ((key_terms, 0), (value_terms, 0), (key_terms, keys), (value_terms, keys))
    ):
        loose[place] = bin_kv[:, place * width : (place + 1) * width]
        for bit in range(2):
            found = loose[place, pl.ds(bit, keys, stride=2), :]
            terms[bit, begin : begin + keys, :] = right_terms(found)

    scale = width**-0.5
    tile = (-1, 8, keys)

    def softmax(scores, mask):
        scores = scores * scale + mask
        raised = jnp.exp(scores - jnp.max(scores, axis=1, keepdims=True))
        return raised * (1.0 / jnp.sum(raised, axis=1, keepdims=True))

    sums[...] = jnp.zeros_like(sums)

    def work(c, carry):
        wait_for(bin_q.at[c], recv2.at[c + 1])
        for inner in range(per_chunk):
            for place in range(3):
                begin = place * chunk_width + inner * width
                loose[place, :keys] = bin_q[c, :, begin : begin + width]
            for bit in range(2):

                def rows(place):
                    return loose[place, pl.ds(bit, half * ROWS, stride=2), :]

                both = jnp.concatenate([left_terms(rows(0)), left_terms(rows(1))], axis=0)
                scores = product(both, key_terms[bit])
                grads = product(left_terms(rows(2)), value_terms[bit])
                top, bottom = scores[: half * ROWS], scores[half * ROWS :]
                plain = top[:, :keys]
                mask = bias[bit]
                weight = softmax(plain, mask)
                weight_other = softmax(bottom[:, keys:], mask)
                part = weight * grads[:, :keys]
                row_dot = jnp.sum(part, axis=1, keepdims=True)
                slope = (part - weight * row_dot) * scale
                head_term = weight_other * grads[:, keys:] - part
                query_term = slope * (bottom[:, :keys] - plain)
                kv_term = slope * (top[:, keys:] - plain) + (weight * grads[:, keys:] - part)
                at = c * per_chunk + inner
                sums[bit, at] = jnp.sum(head_term.reshape(tile), axis=0)
                sums[bit, group + at] = jnp.sum(query_term.reshape(tile), axis=0)
                sums[bit, 2 * group] += jnp.sum(kv_term.reshape(tile), axis=0)
        return carry

    lax.fori_loop(0, CHUNKS, work, 0)

    parts = []
    for bit in range(2):
        lines = [jnp.sum(sums[bit, i], axis=0, keepdims=True) for i in range(2 * group + 1)]
        lines.append(jnp.zeros((width - len(lines), keys), F32))
        lines = jnp.concatenate(lines, axis=0)
        parts.append(
            lax.dot_general(
                members[bit], lines, (((1,), (1,)), ((), ())),
                precision=lax.Precision.HIGHEST, preferred_element_type=F32,
            )
        )
    part_out[...] = jnp.where(own_bit == 0, parts[1], parts[0])
    exchange = pltpu.make_async_remote_copy(
        src_ref=part_out,
        dst_ref=part_in,
        send_sem=small_send.at[1],
        recv_sem=small_recv.at[1],
        device_id=(partner, head),
        device_id_type=MESH,
    )
    exchange.start()
    mine = jnp.where(own_bit == 0, parts[0], parts[1])

    for chunk in range(CHUNKS + 1):
        wait_for(first_of(chunk).at[pl.ds(0, (heads - 1) * rows_here)], send1.at[chunk])
        sent = (n if chunk == 0 else half) - 1
        wait_for(bin_of(chunk).at[pl.ds(0, sent * 8)], send2.at[chunk])

    exchange.wait()
    total = mine + part_in[...]
    head_out[...] = total[:PAIRS_PER_BIN, :group]
    query_out[...] = total[:PAIRS_PER_BIN, group : 2 * group]
    kv_out[...] = total[:PAIRS_PER_BIN, 2 * group : 2 * group + 1]


def shards(n, heads, *arrays):
    segments, plan, offsets = arrays[7:]
    group = arrays[0].shape[1] // arrays[1].shape[1]
    per_chunk = group // CHUNKS
    rows = ROWS * n
    kv_columns, q_columns = 4 * HEAD_SIZE, 3 * per_chunk * HEAD_SIZE
    hbm = pl.BlockSpec(memory_space=pltpu.HBM)
    vmem = pl.BlockSpec(memory_space=pltpu.VMEM)
    return pl.pallas_call(
        functools.partial(kernel, n, heads, group),
        out_shape=[
            jax.ShapeDtypeStruct((PAIRS_PER_BIN, group), F32),
            jax.ShapeDtypeStruct((PAIRS_PER_BIN, group), F32),
            jax.ShapeDtypeStruct((PAIRS_PER_BIN, 1), F32),
        ],
        in_specs=[hbm] * 7 + [vmem] * 3,
        out_specs=[vmem] * 3,
        scratch_shapes=[
            pltpu.VMEM((rows, kv_columns), F32),
            pltpu.VMEM((CHUNKS, rows, q_columns), F32),
            pltpu.VMEM((rows, kv_columns), F32),
            pltpu.VMEM((CHUNKS, rows, q_columns), F32),
            pltpu.VMEM((2 * rows, kv_columns), F32),
            pltpu.VMEM((CHUNKS, rows, q_columns), F32),
            pltpu.VMEM((2, 2 * rows, 6 * HEAD_SIZE), BF16),
            pltpu.VMEM((2, 2 * rows, 6 * HEAD_SIZE), BF16),
            pltpu.VMEM((2, rows // 2, rows), F32),
            pltpu.VMEM((2, 2 * group + 1, 8, rows), F32),
            pltpu.VMEM((4, 2 * rows, HEAD_SIZE), F32),
            pltpu.VMEM((1, rows), jnp.int32),
            pltpu.VMEM((8, HEAD_SIZE), F32),
            pltpu.VMEM((8, HEAD_SIZE), F32),
            pltpu.SemaphoreType.DMA((CHUNKS + 1,)),
            pltpu.SemaphoreType.DMA((CHUNKS + 1,)),
            pltpu.SemaphoreType.DMA((CHUNKS + 1,)),
            pltpu.SemaphoreType.DMA((CHUNKS + 1,)),
            pltpu.SemaphoreType.DMA((2,)),
            pltpu.SemaphoreType.DMA((2,)),
        ],
        compiler_params=pltpu.CompilerParams(
            collective_id=0, has_side_effects=True, vmem_limit_bytes=60 * 1024 * 1024
        ),
    )(*arrays[:7], segments, plan, offsets.reshape(1, -1))


def solution(mesh):
    rows = P(("dp", "head"), None)
    return jax.shard_map(
        functools.partial(shards, mesh.shape["dp"], mesh.shape["head"]),
        mesh=mesh,
        in_specs=(rows,) * 7 + (P("dp", None), P("dp", None), P()),
        out_specs=(P("dp", "head"),) * 3,
        check_vma=False,
    )
```

```python
import functools

import jax
import jax.numpy as jnp
from jax import lax
from jax.experimental import pallas as pl
from jax.experimental.pallas import tpu as pltpu
from jax.sharding import PartitionSpec as P

MESH = pl.DeviceIdType.MESH
F32 = jnp.float32
BF16 = jnp.bfloat16
HEAD_SIZE = 128
PAIRS_PER_BIN = 4
ROWS = 4
SUB = 4
CHUNKS = 4
GROUPS = 4
SKEW = 0
TASKS = (1, 2, 3, 4)


def iota(shape, dim):
    return lax.broadcasted_iota(jnp.int32, shape, dim)


def split3(x):
    high = x.astype(BF16)
    rest = x - high.astype(F32)
    middle = rest.astype(BF16)
    low = (rest - middle.astype(F32)).astype(BF16)
    return high, middle, low


def left_terms(x):
    high, middle, low = split3(x)
    return jnp.concatenate([high, middle, high, middle, high, low], axis=1)


def right_terms(x):
    high, middle, low = split3(x)
    return jnp.concatenate([high, middle, middle, high, low, high], axis=1)


def product(left, right):
    return lax.dot_general(left, right, (((1,), (1,)), ((), ())), preferred_element_type=F32)


def kernel(
    n, heads, group,
    query, key, value, query_other, key_other, value_other, cotangent, segments, plan, offsets,
    head_out, query_out, kv_out,
    first_kv, first_q, send_kv, send_q, ring_kv, bin_q,
    bias, members, starts_in, part_out, part_in,
    send1, recv1_kv, recv1_q, send2, recv2_kv, recv2_q,
    own_send, own_recv, ring_send, ring_recv, small_send, small_recv,
):
    me = lax.axis_index("dp")
    head = lax.axis_index("head")
    ring = n // SUB
    bins = ring // GROUPS
    width = HEAD_SIZE
    rows = ROWS * n
    rows_here = rows // heads
    per_chunk = group // CHUNKS
    planes = 3 * per_chunk
    share = rows // SUB
    part_rows = share // GROUPS
    ring_rows = SUB * part_rows
    reach = ring // 2
    z, sub = me // SUB, me % SUB
    onward = 1 - 2 * (sub % 2)

    def along(steps):
        return (z + steps + ring) % ring

    barrier = pltpu.get_barrier_semaphore()

    def greet(device):
        pl.semaphore_signal(barrier, inc=1, device_id=device, device_id_type=MESH)

    def greet_head(i, carry):
        greet((me, (head + i) % heads))
        return carry

    def greet_sub(i, carry):
        greet((z * SUB + (sub + i) % SUB, head))
        return carry

    def greet_ring(i, carry):
        greet((along(i) * SUB + sub, head))
        return carry

    lax.fori_loop(1, heads, greet_head, 0)
    lax.fori_loop(1, SUB, greet_sub, 0)
    lax.fori_loop(1, ring, greet_ring, 0)
    pl.semaphore_wait(barrier, heads + SUB + ring - 3)

    def remote(source, target, send, receive, device):
        return pltpu.make_async_remote_copy(
            src_ref=source,
            dst_ref=target,
            send_sem=send,
            recv_sem=receive,
            device_id=device,
            device_id_type=MESH,
        )

    def wait_for(ref, semaphore):
        pltpu.make_async_copy(ref, ref, semaphore).wait()

    def sources(chunk, j):
        if chunk == 0:
            for plane, ref in enumerate((key, key_other, value, value_other)):
                yield ref, pl.multiple_of(j * width, width), plane
        else:
            for place, ref in enumerate((query, query_other, cotangent)):
                for inner in range(per_chunk):
                    at = j * (group * width) + ((chunk - 1) * per_chunk + inner) * width
                    yield ref, pl.multiple_of(at, width), place * per_chunk + inner

    def first_of(chunk):
        return first_kv if chunk == 0 else first_q.at[chunk - 1]

    def start_first(chunk):
        at = pl.multiple_of(head * rows_here, 8)
        for some in range(4 if chunk == 0 else 1):

            def pieces(j):
                for ref, column, plane in sources(chunk, j):
                    if chunk or plane == some:
                        arrived = recv1_q.at[chunk - 1] if chunk else recv1_kv.at[plane]
                        target = first_of(chunk).at[plane, pl.ds(at, rows_here), :]
                        yield ref.at[:, pl.ds(column, width)], target, arrived

            def to(i, carry):
                j = (head + i) % heads
                for source, target, arrived in pieces(j):
                    remote(source, target, send1.at[chunk], arrived, (me, j)).start()
                return carry

            lax.fori_loop(1, heads, to, 0)
            for source, target, arrived in pieces(head):
                pltpu.make_async_copy(source, target, arrived).start()

    def spread(source, target, send, arrived):
        for i in range(1, SUB):
            to = (sub + i) % SUB
            remote(source(to), target, send, arrived, (z * SUB + to, head)).start()
        pltpu.make_async_copy(source(sub), target, arrived).start()

    start_first(0)

    segment = segments[...]
    lane = iota((1, width), 1)
    starts = jnp.zeros((1, width), F32)
    for g in range(1, PAIRS_PER_BIN):
        start = jnp.sum(jnp.where(segment < g, 1.0, 0.0), axis=1, keepdims=True)
        starts = jnp.where(lane == g, start, starts)
    starts_in[z] = jnp.broadcast_to(starts, (8, width))

    def tell(i, carry):
        remote(
            starts_in.at[z], starts_in.at[z], small_send.at[0], small_recv.at[0],
            (along(i) * SUB + sub, head),
        ).start()
        return carry

    lax.fori_loop(1, ring, tell, 0)

    off_row = offsets[...].astype(F32)
    plan_row = plan[...].astype(F32)
    square = (n, n)
    same = iota(square, 0) == iota(square, 1)
    lanes = iota(square, 1).astype(F32)
    off_column = jnp.sum(jnp.where(same, off_row, 0.0), axis=1, keepdims=True)
    plan_column = jnp.sum(jnp.where(same, plan_row, 0.0), axis=1, keepdims=True)
    distance = jnp.sum(jnp.where(plan_column == lanes, off_row, 0.0), axis=1, keepdims=True)
    target = me.astype(F32) + distance
    target = jnp.where(target >= n, target - n, target)
    wide = (n, rows)
    one = (1, rows)
    block = iota(wide, 1) // ROWS
    target_row = jnp.sum(jnp.where(iota(wide, 0) == block, target, 0.0), axis=0, keepdims=True)
    key_in = target_row * ROWS + (iota(one, 1) % ROWS).astype(F32)
    out = iota((rows, 1), 0)
    to_sub, inside = out // share, out % share
    kv_bin = inside // part_rows * bins + inside % bins
    kv_row = inside % part_rows // bins

    def ordering(bin_z, row):
        key_to = ((bin_z * SUB + to_sub) * ROWS + row).astype(F32)
        return jnp.where(key_to == key_in, 1.0, 0.0).astype(BF16)

    def moved(order, block):
        high, middle, low = split3(block)
        result = jnp.dot(order, high, preferred_element_type=F32)
        result += jnp.dot(order, middle, preferred_element_type=F32)
        return result + jnp.dot(order, low, preferred_element_type=F32)

    order_kv = ordering(kv_bin, kv_row)
    order_q = ordering(inside % ring, inside // ring)

    def second_kv(plane):
        wait_for(first_kv.at[plane], recv1_kv.at[plane])
        send_kv[plane] = moved(order_kv, first_kv[plane]).reshape(SUB, GROUPS, part_rows, width)
        at = pl.multiple_of(z * ring_rows + sub * part_rows, 8)
        target = ring_kv.at[:, plane, pl.ds(at, part_rows), :]
        spread(lambda to: send_kv.at[plane, to], target, send2.at[0], recv2_kv.at[plane])

    def second_q(c):
        wait_for(first_q.at[c], recv1_q.at[c])
        for plane in range(0, planes, 2):
            both = jnp.concatenate([first_q[c, plane], first_q[c, plane + 1]], axis=1)
            both = moved(order_q, both)
            send_q[c, plane] = both[:, :width]
            send_q[c, plane + 1] = both[:, width:]
        target = bin_q.at[c, :, pl.ds(pl.multiple_of(sub * share, 8), share), :]
        spread(
            lambda to: send_q.at[c, :, pl.ds(pl.multiple_of(to * share, 8), share), :],
            target, send2.at[c + 1], recv2_q.at[c],
        )

    def plane_of(plane, origin):
        return ring_kv.at[:, plane, pl.ds(pl.multiple_of(origin * ring_rows, 8), ring_rows), :]

    def piece(g, origin):
        return ring_kv.at[g, :, pl.ds(pl.multiple_of(origin * ring_rows, 8), ring_rows), :]

    def turn_of(way):
        return onward * (1 - 2 * way)

    def next_of(way):
        return (along(turn_of(way)) * SUB + sub, head)

    def send_own(plane):
        held = plane_of(plane, z)
        wait_for(held, recv2_kv.at[plane])
        for way in range(2):
            remote(held, held, own_send.at[way], own_recv.at[way, plane], next_of(way)).start()

    def receive_first():
        for way in range(2):
            for plane in range(4):
                wait_for(plane_of(plane, along(-turn_of(way))), own_recv.at[way, plane])

    def ring_step(g, step):
        for way in range(2):
            if step > reach - way:
                continue
            held = piece(g, along(-turn_of(way) * step))
            if step > 1:
                wait_for(held, ring_recv.at[way, g, step - 2])
            if step < reach - way:
                remote(
                    held, held, ring_send.at[way, g], ring_recv.at[way, g, step - 1], next_of(way)
                ).start()

    second_kv(0)
    second_kv(1)
    send_own(0)
    second_kv(2)
    send_own(1)
    second_kv(3)
    start_first(1)
    send_own(2)
    send_own(3)
    start_first(2)

    q_index = iota((SUB * ROWS, 1), 0)
    q_source = z * SUB + q_index // ROWS
    k_source = iota(one, 1) // ROWS

    def describe(at, carry):
        which = at * SUB + sub
        starts = starts_in[at]
        k_distance = ((which - k_source + n) % n).astype(F32)
        k_slot = jnp.sum(
            jnp.where(off_column == k_distance, iota(wide, 0).astype(F32), 0.0), axis=0, keepdims=True
        )
        k_place = k_slot * ROWS + (iota(one, 1) % ROWS).astype(F32)
        q_distance = ((which - q_source + n) % n).astype(F32)
        tall = (SUB * ROWS, n)
        q_slot = jnp.sum(
            jnp.where(off_row == q_distance, iota(tall, 1).astype(F32), 0.0), axis=1, keepdims=True
        )
        q_place = q_slot * ROWS + (q_index % ROWS).astype(F32)
        begin = jnp.zeros_like(q_place)
        k_segment = jnp.zeros_like(k_place)
        for g in range(1, PAIRS_PER_BIN):
            start = starts[:1, g : g + 1]
            begin = jnp.where(q_place >= start, start, begin)
            k_segment += jnp.where(k_place >= start, 1.0, 0.0)
        allowed = jnp.logical_and(k_place <= q_place, k_place >= begin)
        bias[at] = jnp.where(allowed, 0.0, -jnp.inf)
        members[at] = jnp.where(k_segment == iota((8, rows), 0).astype(F32), 1.0, 0.0)
        return carry

    scale = width**-0.5

    def softmax(scores, mask):
        scores = scores * scale + mask
        raised = jnp.exp(scores - jnp.max(scores, axis=1, keepdims=True))
        return raised * (1.0 / jnp.sum(raised, axis=1, keepdims=True))

    def work(at):
        g, inner_bin = at // bins, at % bins

        def keys(plane):
            return ring_kv[g, plane, pl.ds(inner_bin, rows, stride=bins), :]

        def queries(place):
            found = [
                bin_q[i // per_chunk, place * per_chunk + i % per_chunk, pl.ds(at, SUB * ROWS, stride=ring), :]
                for i in range(group)
            ]
            return jnp.concatenate(found, axis=0)

        key_terms = jnp.concatenate([right_terms(keys(0)), right_terms(keys(1))], axis=0)
        value_terms = jnp.concatenate([right_terms(keys(2)), right_terms(keys(3))], axis=0)
        both = jnp.concatenate([left_terms(queries(0)), left_terms(queries(1))], axis=0)
        scores = product(both, key_terms)
        grads = product(left_terms(queries(2)), value_terms)
        count = group * SUB * ROWS
        top, bottom = scores[:count], scores[count:]
        plain = top[:, :rows]
        mask = jnp.concatenate([bias[at]] * group, axis=0)
        weight = softmax(plain, mask)
        weight_other = softmax(bottom[:, rows:], mask)
        part = weight * grads[:, :rows]
        row_dot = jnp.sum(part, axis=1, keepdims=True)
        slope = (part - weight * row_dot) * scale
        head_term = weight_other * grads[:, rows:] - part
        query_term = slope * (bottom[:, :rows] - plain)
        kv_term = slope * (top[:, rows:] - plain) + (weight * grads[:, rows:] - part)
        by_head = (group, SUB * ROWS, rows)
        sums = jnp.concatenate(
            [
                jnp.sum(head_term.reshape(by_head), axis=1),
                jnp.sum(query_term.reshape(by_head), axis=1),
                jnp.sum(kv_term.reshape(-1, 8, rows), axis=0),
            ],
            axis=0,
        )
        found = jnp.zeros((2 * group + 8, width), F32)
        member = members[at]
        for g in range(PAIRS_PER_BIN):
            line = jnp.sum(sums * member[g : g + 1], axis=1, keepdims=True)
            found = jnp.where(lane == g, line, found)
        part_out[at] = found

        @pl.when(at != z)
        def _():
            remote(
                part_out.at[at], part_in.at[z], small_send.at[1], small_recv.at[1], (at * SUB + sub, head)
            ).start()

        @pl.when(at == z)
        def _():
            pltpu.make_async_copy(part_out.at[at], part_in.at[z], small_recv.at[1]).start()

    others = starts_in.at[pl.ds(0, ring - 1)]
    wait_for(others, small_send.at[0])
    wait_for(others, small_recv.at[0])
    lax.fori_loop(0, ring, describe, 0)
    receive_first()
    for tau in range(1, reach):
        for g in range(GROUPS):
            if tau - SKEW * g > 0:
                ring_step(g, tau - SKEW * g)
        for c, when in enumerate(TASKS):
            if tau == when:
                second_q(c)
                if c + 3 <= CHUNKS:
                    start_first(c + 3)
    for c in range(CHUNKS):
        wait_for(bin_q.at[c], recv2_q.at[c])
    done = [reach - 1 - SKEW * g for g in range(GROUPS)]
    for g in range(GROUPS):
        while done[g] < reach:
            for i in range(g, GROUPS if SKEW else g + 1):
                done[i] += 1
                if done[i] > 0:
                    ring_step(i, done[i])

        def one_bin(i, carry):
            work(g * bins + i)
            return carry

        lax.fori_loop(0, bins, one_bin, 0)

    for chunk in range(CHUNKS + 1):
        wait_for(first_of(chunk).at[:, pl.ds(0, (heads - 1) * rows_here), :], send1.at[chunk])
        wait_for(first_of(chunk).at[:, pl.ds(0, (SUB - 1) * share), :], send2.at[chunk])
    for g in range(GROUPS):
        for way in range(2):
            wait_for(ring_kv.at[g, :, pl.ds(0, (reach - way - 1) * ring_rows), :], ring_send.at[way, g])
    for way in range(2):
        wait_for(ring_kv.at[:, :, pl.ds(0, ring_rows), :], own_send.at[way])
    wait_for(part_out.at[pl.ds(0, ring - 1)], small_send.at[1])
    wait_for(part_in, small_recv.at[1])
    total = jnp.sum(part_in[...], axis=0)
    eye = iota((group, group), 0) == iota((group, group), 1)
    for g in range(PAIRS_PER_BIN):
        column = total[:, g : g + 1]
        head_out[g : g + 1, :] = jnp.sum(jnp.where(eye, column[:group], 0.0), axis=0, keepdims=True)
        query_out[g : g + 1, :] = jnp.sum(
            jnp.where(eye, column[group : 2 * group], 0.0), axis=0, keepdims=True
        )
        kv_out[g : g + 1, :] = jnp.sum(column[2 * group :], axis=0, keepdims=True)


def shards(n, heads, *arrays):
    segments, plan, offsets = arrays[7:]
    group = arrays[0].shape[1] // arrays[1].shape[1]
    planes = 3 * group // CHUNKS
    rows = ROWS * n
    ring = n // SUB
    hbm = pl.BlockSpec(memory_space=pltpu.HBM)
    vmem = pl.BlockSpec(memory_space=pltpu.VMEM)
    dma = pltpu.SemaphoreType.DMA
    return pl.pallas_call(
        functools.partial(kernel, n, heads, group),
        out_shape=[
            jax.ShapeDtypeStruct((PAIRS_PER_BIN, group), F32),
            jax.ShapeDtypeStruct((PAIRS_PER_BIN, group), F32),
            jax.ShapeDtypeStruct((PAIRS_PER_BIN, 1), F32),
        ],
        in_specs=[hbm] * 7 + [vmem] * 3,
        out_specs=[vmem] * 3,
        scratch_shapes=[
            pltpu.VMEM((4, rows, HEAD_SIZE), F32),
            pltpu.VMEM((CHUNKS, planes, rows, HEAD_SIZE), F32),
            pltpu.VMEM((4, SUB, GROUPS, rows // SUB // GROUPS, HEAD_SIZE), F32),
            pltpu.VMEM((CHUNKS, planes, rows, HEAD_SIZE), F32),
            pltpu.VMEM((GROUPS, 4, ring * rows // GROUPS, HEAD_SIZE), F32),
            pltpu.VMEM((CHUNKS, planes, rows, HEAD_SIZE), F32),
            pltpu.VMEM((ring, SUB * ROWS, rows), F32),
            pltpu.VMEM((ring, 8, rows), F32),
            pltpu.VMEM((ring, 8, HEAD_SIZE), F32),
            pltpu.VMEM((ring, 2 * group + 8, HEAD_SIZE), F32),
            pltpu.VMEM((ring, 2 * group + 8, HEAD_SIZE), F32),
            dma((CHUNKS + 1,)),
            dma((4,)),
            dma((CHUNKS,)),
            dma((CHUNKS + 1,)),
            dma((4,)),
            dma((CHUNKS,)),
            dma((2,)),
            dma((2, 4)),
            dma((2, GROUPS)),
            dma((2, GROUPS, ring // 2 - 1)),
            dma((2,)),
            dma((2,)),
        ],
        compiler_params=pltpu.CompilerParams(
            collective_id=0, has_side_effects=True, vmem_limit_bytes=60 * 1024 * 1024
        ),
    )(*arrays[:7], segments, plan, offsets.reshape(1, -1))


def solution(mesh):
    rows = P(("dp", "head"), None)
    return jax.shard_map(
        functools.partial(shards, mesh.shape["dp"], mesh.shape["head"]),
        mesh=mesh,
        in_specs=(rows,) * 7 + (P("dp", None), P("dp", None), P()),
        out_specs=(P("dp", "head"),) * 3,
        check_vma=False,
    )
```

```python
import functools

import jax
import jax.numpy as jnp
from jax import lax
from jax.experimental import pallas as pl
from jax.experimental.pallas import tpu as pltpu
from jax.sharding import PartitionSpec as P

MESH = pl.DeviceIdType.MESH
F32 = jnp.float32
BF16 = jnp.bfloat16
HEAD_SIZE = 128
PAIRS_PER_BIN = 4
ROWS = 4
SUB = 4
CHUNKS = 4
GROUPS = 8
SKEW = 0
TASKS = (1, 2, 3, 4)


def iota(shape, dim):
    return lax.broadcasted_iota(jnp.int32, shape, dim)


def split3(x):
    high = x.astype(BF16)
    rest = x - high.astype(F32)
    middle = rest.astype(BF16)
    low = (rest - middle.astype(F32)).astype(BF16)
    return high, middle, low


def left_terms(x):
    high, middle, low = split3(x)
    return jnp.concatenate([high, middle, high, middle, high, low], axis=1)


def right_terms(x):
    high, middle, low = split3(x)
    return jnp.concatenate([high, middle, middle, high, low, high], axis=1)


def product(left, right):
    return lax.dot_general(left, right, (((1,), (1,)), ((), ())), preferred_element_type=F32)


def kernel(
    n, heads, group,
    query, key, value, query_other, key_other, value_other, cotangent, segments, plan, offsets,
    out_ref,
    first_kv, first_q, send_kv, send_q, ring_kv, bin_q,
    bias, members, starts_in, part_out, part_in,
    send1, recv1_kv, recv1_q, send2, recv2_kv, recv2_q,
    own_send, own_recv, ring_send, ring_recv, small_send, small_recv,
):
    me = lax.axis_index("dp")
    head = lax.axis_index("head")
    ring = n // SUB
    bins = ring // GROUPS
    width = HEAD_SIZE
    rows = ROWS * n
    rows_here = rows // heads
    per_chunk = group // CHUNKS
    planes = 3 * per_chunk
    share = rows // SUB
    part_rows = share // GROUPS
    ring_rows = SUB * part_rows
    reach = ring // 2
    z, sub = me // SUB, me % SUB

    def along(steps):
        return (z + steps + ring) % ring

    barrier = pltpu.get_barrier_semaphore()

    def greet(device):
        pl.semaphore_signal(barrier, inc=1, device_id=device, device_id_type=MESH)

    def greet_head(i, carry):
        greet((me, (head + i) % heads))
        return carry

    def greet_sub(i, carry):
        greet((z * SUB + (sub + i) % SUB, head))
        return carry

    def greet_ring(i, carry):
        greet((along(i) * SUB + sub, head))
        return carry

    lax.fori_loop(1, heads, greet_head, 0)
    lax.fori_loop(1, SUB, greet_sub, 0)
    lax.fori_loop(1, ring, greet_ring, 0)
    pl.semaphore_wait(barrier, heads + SUB + ring - 3)

    def remote(source, target, send, receive, device):
        return pltpu.make_async_remote_copy(
            src_ref=source,
            dst_ref=target,
            send_sem=send,
            recv_sem=receive,
            device_id=device,
            device_id_type=MESH,
        )

    def wait_for(ref, semaphore):
        pltpu.make_async_copy(ref, ref, semaphore).wait()

    def sources(chunk, j):
        if chunk == 0:
            for plane, ref in enumerate((key, key_other, value, value_other)):
                yield ref, pl.multiple_of(j * width, width), plane
        else:
            for place, ref in enumerate((query, query_other, cotangent)):
                for inner in range(per_chunk):
                    at = j * (group * width) + ((chunk - 1) * per_chunk + inner) * width
                    yield ref, pl.multiple_of(at, width), place * per_chunk + inner

    def first_of(chunk):
        return first_kv if chunk == 0 else first_q.at[chunk - 1]

    def start_first(chunk):
        at = pl.multiple_of(head * rows_here, 8)
        for some in range(4 if chunk == 0 else 1):

            def pieces(j):
                for ref, column, plane in sources(chunk, j):
                    if chunk or plane == some:
                        arrived = recv1_q.at[chunk - 1] if chunk else recv1_kv.at[plane]
                        target = first_of(chunk).at[plane, pl.ds(at, rows_here), :]
                        yield ref.at[:, pl.ds(column, width)], target, arrived

            def to(i, carry):
                j = (head + i) % heads
                for source, target, arrived in pieces(j):
                    remote(source, target, send1.at[chunk], arrived, (me, j)).start()
                return carry

            lax.fori_loop(1, heads, to, 0)
            for source, target, arrived in pieces(head):
                pltpu.make_async_copy(source, target, arrived).start()

    def spread(source, target, send, arrived):
        for i in range(1, SUB):
            to = (sub + i) % SUB
            remote(source(to), target, send, arrived, (z * SUB + to, head)).start()
        pltpu.make_async_copy(source(sub), target, arrived).start()

    start_first(0)

    segment = segments[...]
    lane = iota((1, width), 1)
    starts = jnp.zeros((1, width), F32)
    for g in range(1, PAIRS_PER_BIN):
        start = jnp.sum(jnp.where(segment < g, 1.0, 0.0), axis=1, keepdims=True)
        starts = jnp.where(lane == g, start, starts)
    starts_in[z] = jnp.broadcast_to(starts, (8, width))

    def tell(i, carry):
        remote(
            starts_in.at[z], starts_in.at[z], small_send.at[0], small_recv.at[0],
            (along(i) * SUB + sub, head),
        ).start()
        return carry

    lax.fori_loop(1, ring, tell, 0)

    off_row = offsets[...].astype(F32)
    plan_row = plan[...].astype(F32)
    square = (n, n)
    same = iota(square, 0) == iota(square, 1)
    lanes = iota(square, 1).astype(F32)
    off_column = jnp.sum(jnp.where(same, off_row, 0.0), axis=1, keepdims=True)
    plan_column = jnp.sum(jnp.where(same, plan_row, 0.0), axis=1, keepdims=True)
    distance = jnp.sum(jnp.where(plan_column == lanes, off_row, 0.0), axis=1, keepdims=True)
    target = me.astype(F32) + distance
    target = jnp.where(target >= n, target - n, target)
    wide = (n, rows)
    one = (1, rows)
    block = iota(wide, 1) // ROWS
    target_row = jnp.sum(jnp.where(iota(wide, 0) == block, target, 0.0), axis=0, keepdims=True)
    key_in = target_row * ROWS + (iota(one, 1) % ROWS).astype(F32)
    out = iota((rows, 1), 0)
    to_sub, inside = out // share, out % share
    kv_bin = inside // part_rows * bins + inside % bins
    kv_row = inside % part_rows // bins

    def ordering(bin_z, row):
        key_to = ((bin_z * SUB + to_sub) * ROWS + row).astype(F32)
        return jnp.where(key_to == key_in, 1.0, 0.0).astype(BF16)

    def moved(order, block):
        high, middle, low = split3(block)
        result = jnp.dot(order, high, preferred_element_type=F32)
        result += jnp.dot(order, middle, preferred_element_type=F32)
        return result + jnp.dot(order, low, preferred_element_type=F32)

    order_kv = ordering(kv_bin, kv_row)
    order_q = ordering(inside % ring, inside // ring)

    def second_kv(plane):
        wait_for(first_kv.at[plane], recv1_kv.at[plane])
        send_kv[plane] = moved(order_kv, first_kv[plane]).reshape(SUB, GROUPS, part_rows, width)
        at = pl.multiple_of(z * ring_rows + sub * part_rows, 8)
        target = ring_kv.at[:, plane, pl.ds(at, part_rows), :]
        spread(lambda to: send_kv.at[plane, to], target, send2.at[0], recv2_kv.at[plane])

    def second_q(c):
        wait_for(first_q.at[c], recv1_q.at[c])
        for plane in range(0, planes, 2):
            both = jnp.concatenate([first_q[c, plane], first_q[c, plane + 1]], axis=1)
            both = moved(order_q, both)
            send_q[c, plane] = both[:, :width]
            send_q[c, plane + 1] = both[:, width:]
        target = bin_q.at[c, :, pl.ds(pl.multiple_of(sub * share, 8), share), :]
        spread(
            lambda to: send_q.at[c, :, pl.ds(pl.multiple_of(to * share, 8), share), :],
            target, send2.at[c + 1], recv2_q.at[c],
        )

    def plane_of(plane, origin):
        return ring_kv.at[:, plane, pl.ds(pl.multiple_of(origin * ring_rows, 8), ring_rows), :]

    def piece(g, origin):
        return ring_kv.at[g, :, pl.ds(pl.multiple_of(origin * ring_rows, 8), ring_rows), :]

    def turn_of(way):
        return 1 - 2 * way

    def next_of(way):
        return (along(turn_of(way)) * SUB + sub, head)

    def send_own(plane):
        wait_for(plane_of(plane, z), recv2_kv.at[plane])
        for place in range(GROUPS if plane == 3 else 1):
            held = piece(place, z).at[3] if plane == 3 else plane_of(plane, z)
            for way in range(2):
                arrived = own_recv.at[way, plane + place]
                remote(held, held, own_send.at[way], arrived, next_of(way)).start()

    def receive_first():
        for way in range(2):
            for plane in range(3):
                wait_for(plane_of(plane, along(-turn_of(way))), own_recv.at[way, plane])

    def ring_step(g, step):
        for way in range(2):
            held = piece(g, along(-turn_of(way) * step))
            half = held.at[pl.ds(2 * way, 2)]
            if step == 1:
                wait_for(held.at[3], own_recv.at[way, 3 + g])
            else:
                wait_for(half if step == reach else held, ring_recv.at[way, g, step - 2])
            if step < reach:
                going = half if step == reach - 1 else held
                remote(
                    going, going, ring_send.at[way, g], ring_recv.at[way, g, step - 1], next_of(way)
                ).start()

    second_kv(0)
    second_kv(1)
    send_own(0)
    second_kv(2)
    send_own(1)
    second_kv(3)
    start_first(1)
    send_own(2)
    send_own(3)
    start_first(2)
    start_first(3)
    start_first(4)

    q_index = iota((SUB * ROWS, 1), 0)
    q_source = z * SUB + q_index // ROWS
    k_source = iota(one, 1) // ROWS

    def describe(at, carry):
        which = at * SUB + sub
        starts = starts_in[at]
        k_distance = ((which - k_source + n) % n).astype(F32)
        k_slot = jnp.sum(
            jnp.where(off_column == k_distance, iota(wide, 0).astype(F32), 0.0), axis=0, keepdims=True
        )
        k_place = k_slot * ROWS + (iota(one, 1) % ROWS).astype(F32)
        q_distance = ((which - q_source + n) % n).astype(F32)
        tall = (SUB * ROWS, n)
        q_slot = jnp.sum(
            jnp.where(off_row == q_distance, iota(tall, 1).astype(F32), 0.0), axis=1, keepdims=True
        )
        q_place = q_slot * ROWS + (q_index % ROWS).astype(F32)
        begin = jnp.zeros_like(q_place)
        k_segment = jnp.zeros_like(k_place)
        for g in range(1, PAIRS_PER_BIN):
            start = starts[:1, g : g + 1]
            begin = jnp.where(q_place >= start, start, begin)
            k_segment += jnp.where(k_place >= start, 1.0, 0.0)
        allowed = jnp.logical_and(k_place <= q_place, k_place >= begin)
        bias[at] = jnp.where(allowed, 0.0, -jnp.inf)
        members[at] = jnp.where(k_segment == iota((8, rows), 0).astype(F32), 1.0, 0.0)
        return carry

    scale = width**-0.5

    def softmax(scores, mask):
        scores = scores * scale + mask
        raised = jnp.exp(scores - jnp.max(scores, axis=1, keepdims=True))
        return raised * (1.0 / jnp.sum(raised, axis=1, keepdims=True))

    def work(at):
        g, inner_bin = at // bins, at % bins

        def keys(plane):
            return ring_kv[g, plane, pl.ds(inner_bin, rows, stride=bins), :]

        def queries(place):
            found = [
                bin_q[i // per_chunk, place * per_chunk + i % per_chunk, pl.ds(at, SUB * ROWS, stride=ring), :]
                for i in range(group)
            ]
            return jnp.concatenate(found, axis=0)

        key_terms = jnp.concatenate([right_terms(keys(0)), right_terms(keys(1))], axis=0)
        value_terms = jnp.concatenate([right_terms(keys(2)), right_terms(keys(3))], axis=0)
        both = jnp.concatenate([left_terms(queries(0)), left_terms(queries(1))], axis=0)
        scores = product(both, key_terms)
        grads = product(left_terms(queries(2)), value_terms)
        count = group * SUB * ROWS
        top, bottom = scores[:count], scores[count:]
        plain = top[:, :rows]
        mask = jnp.concatenate([bias[at]] * group, axis=0)
        weight = softmax(plain, mask)
        weight_other = softmax(bottom[:, rows:], mask)
        part = weight * grads[:, :rows]
        row_dot = jnp.sum(part, axis=1, keepdims=True)
        slope = (part - weight * row_dot) * scale
        head_term = weight_other * grads[:, rows:] - part
        query_term = slope * (bottom[:, :rows] - plain)
        kv_term = slope * (top[:, rows:] - plain) + (weight * grads[:, rows:] - part)
        by_head = (group, SUB * ROWS, rows)
        sums = jnp.concatenate(
            [
                jnp.sum(head_term.reshape(by_head), axis=1),
                jnp.sum(query_term.reshape(by_head), axis=1),
                jnp.sum(kv_term.reshape(-1, 8, rows), axis=0),
            ],
            axis=0,
        )
        found = jnp.zeros((2 * group + 8, width), F32)
        member = members[at]
        for g in range(PAIRS_PER_BIN):
            line = jnp.sum(sums * member[g : g + 1], axis=1, keepdims=True)
            found = jnp.where(lane == g, line, found)
        part_out[at] = found

        @pl.when(at != z)
        def _():
            remote(
                part_out.at[at], part_in.at[z], small_send.at[1], small_recv.at[1], (at * SUB + sub, head)
            ).start()

        @pl.when(at == z)
        def _():
            pltpu.make_async_copy(part_out.at[at], part_in.at[z], small_recv.at[1]).start()

    others = starts_in.at[pl.ds(0, ring - 1)]
    wait_for(others, small_send.at[0])
    wait_for(others, small_recv.at[0])
    lax.fori_loop(0, ring, describe, 0)
    receive_first()
    for tau in range(1, reach):
        for g in range(GROUPS):
            if tau - SKEW * g > 0:
                ring_step(g, tau - SKEW * g)
        for c, when in enumerate(TASKS):
            if tau == when:
                second_q(c)
    for c in range(CHUNKS):
        wait_for(bin_q.at[c], recv2_q.at[c])
    done = [reach - 1 - SKEW * g for g in range(GROUPS)]
    for g in range(GROUPS):
        while done[g] < reach:
            for i in range(g, GROUPS if SKEW else g + 1):
                done[i] += 1
                if done[i] > 0:
                    ring_step(i, done[i])

        def one_bin(i, carry):
            work(g * bins + i)
            return carry

        lax.fori_loop(0, bins, one_bin, 0)

    for chunk in range(CHUNKS + 1):
        wait_for(first_of(chunk).at[:, pl.ds(0, (heads - 1) * rows_here), :], send1.at[chunk])
        wait_for(first_of(chunk).at[:, pl.ds(0, (SUB - 1) * share), :], send2.at[chunk])
    for g in range(GROUPS):
        for way in range(2):
            wait_for(ring_kv.at[g, pl.ds(0, 2), pl.ds(0, (2 * reach - 3) * ring_rows), :], ring_send.at[way, g])
    for way in range(2):
        wait_for(ring_kv.at[:, :, pl.ds(0, ring_rows), :], own_send.at[way])
    wait_for(part_out.at[pl.ds(0, ring - 1)], small_send.at[1])
    wait_for(part_in, small_recv.at[1])
    total = jnp.sum(part_in[...], axis=0)
    shape = (2 * group + 8, width)
    eye = iota(shape, 0) == iota(shape, 1)
    for g in range(PAIRS_PER_BIN):
        line = jnp.where(eye, total[:, g : g + 1], 0.0)
        out_ref[g : g + 1, :] = jnp.sum(line, axis=0, keepdims=True)
    keyed = jnp.sum(total[2 * group :], axis=0, keepdims=True)
    out_ref[PAIRS_PER_BIN:, :] = jnp.broadcast_to(keyed, (8 - PAIRS_PER_BIN, width))


def shards(n, heads, *arrays):
    segments, plan, offsets = arrays[7:]
    group = arrays[0].shape[1] // arrays[1].shape[1]
    planes = 3 * group // CHUNKS
    rows = ROWS * n
    ring = n // SUB
    hbm = pl.BlockSpec(memory_space=pltpu.HBM)
    vmem = pl.BlockSpec(memory_space=pltpu.VMEM)
    dma = pltpu.SemaphoreType.DMA
    packed = pl.pallas_call(
        functools.partial(kernel, n, heads, group),
        out_shape=jax.ShapeDtypeStruct((8, HEAD_SIZE), F32),
        in_specs=[hbm] * 7 + [vmem] * 3,
        out_specs=vmem,
        scratch_shapes=[
            pltpu.VMEM((4, rows, HEAD_SIZE), F32),
            pltpu.VMEM((CHUNKS, planes, rows, HEAD_SIZE), F32),
            pltpu.VMEM((4, SUB, GROUPS, rows // SUB // GROUPS, HEAD_SIZE), F32),
            pltpu.VMEM((CHUNKS, planes, rows, HEAD_SIZE), F32),
            pltpu.VMEM((GROUPS, 4, ring * rows // GROUPS, HEAD_SIZE), F32),
            pltpu.VMEM((CHUNKS, planes, rows, HEAD_SIZE), F32),
            pltpu.VMEM((ring, SUB * ROWS, rows), F32),
            pltpu.VMEM((ring, 8, rows), F32),
            pltpu.VMEM((ring, 8, HEAD_SIZE), F32),
            pltpu.VMEM((ring, 2 * group + 8, HEAD_SIZE), F32),
            pltpu.VMEM((ring, 2 * group + 8, HEAD_SIZE), F32),
            dma((CHUNKS + 1,)),
            dma((4,)),
            dma((CHUNKS,)),
            dma((CHUNKS + 1,)),
            dma((4,)),
            dma((CHUNKS,)),
            dma((2,)),
            dma((2, 3 + GROUPS)),
            dma((2, GROUPS)),
            dma((2, GROUPS, ring // 2 - 1)),
            dma((2,)),
            dma((2,)),
        ],
        compiler_params=pltpu.CompilerParams(
            collective_id=0, has_side_effects=True, vmem_limit_bytes=60 * 1024 * 1024
        ),
    )(*arrays[:7], segments, plan, offsets.reshape(1, -1))
    found = packed[:PAIRS_PER_BIN]
    keyed = packed[PAIRS_PER_BIN : PAIRS_PER_BIN + 1, :PAIRS_PER_BIN]
    return found[:, :group], found[:, group : 2 * group], keyed.reshape(-1, 1)


def solution(mesh):
    rows = P(("dp", "head"), None)
    return jax.shard_map(
        functools.partial(shards, mesh.shape["dp"], mesh.shape["head"]),
        mesh=mesh,
        in_specs=(rows,) * 7 + (P("dp", None), P("dp", None), P()),
        out_specs=(P("dp", "head"),) * 3,
        check_vma=False,
    )
```

```python
import functools

import jax
import jax.numpy as jnp
from jax import lax
from jax.experimental import pallas as pl
from jax.experimental.pallas import tpu as pltpu
from jax.sharding import PartitionSpec as P

MESH = pl.DeviceIdType.MESH
F32 = jnp.float32
BF16 = jnp.bfloat16
HEAD_SIZE = 128
PAIRS_PER_BIN = 4
ROWS = 4
SUB = 4
CHUNKS = 4
GROUPS = 8
SKEW = 0
TASKS = (1, 2, 3, 4)


def iota(shape, dim):
    return lax.broadcasted_iota(jnp.int32, shape, dim)


def split3(x):
    high = x.astype(BF16)
    rest = x - high.astype(F32)
    middle = rest.astype(BF16)
    low = (rest - middle.astype(F32)).astype(BF16)
    return high, middle, low


def left_terms(x):
    high, middle, low = split3(x)
    return jnp.concatenate([high, middle, high, middle, high, low], axis=1)


def right_terms(x):
    high, middle, low = split3(x)
    return jnp.concatenate([high, middle, middle, high, low, high], axis=1)


def product(left, right):
    return lax.dot_general(left, right, (((1,), (1,)), ((), ())), preferred_element_type=F32)


def kernel(
    n, heads, group,
    query, key, value, query_other, key_other, value_other, cotangent, segments, plan, offsets,
    out_ref,
    first_kv, first_q, send_kv, send_q, ring_kv, bin_q,
    bias, members, starts_in, part_out, part_in,
    send1, recv1_kv, recv1_q, send2, recv2_kv, recv2_q,
    own_send, own_recv, ring_send, ring_recv, small_send, small_recv,
):
    me = lax.axis_index("dp")
    head = lax.axis_index("head")
    ring = n // SUB
    bins = ring // GROUPS
    width = HEAD_SIZE
    rows = ROWS * n
    rows_here = rows // heads
    per_chunk = group // CHUNKS
    planes = 3 * per_chunk
    share = rows // SUB
    part_rows = share // GROUPS
    ring_rows = SUB * part_rows
    reach = ring // 2
    z, sub = me // SUB, me % SUB

    def along(steps):
        return (z + steps + ring) % ring

    barrier = pltpu.get_barrier_semaphore()

    def greet(device):
        pl.semaphore_signal(barrier, inc=1, device_id=device, device_id_type=MESH)

    def greet_head(i, carry):
        greet((me, (head + i) % heads))
        return carry

    def greet_sub(i, carry):
        greet((z * SUB + (sub + i) % SUB, head))
        return carry

    def greet_ring(i, carry):
        greet((along(i) * SUB + sub, head))
        return carry

    lax.fori_loop(1, heads, greet_head, 0)
    lax.fori_loop(1, SUB, greet_sub, 0)
    lax.fori_loop(1, ring, greet_ring, 0)
    pl.semaphore_wait(barrier, heads + SUB + ring - 3)

    def remote(source, target, send, receive, device):
        return pltpu.make_async_remote_copy(
            src_ref=source,
            dst_ref=target,
            send_sem=send,
            recv_sem=receive,
            device_id=device,
            device_id_type=MESH,
        )

    def wait_for(ref, semaphore):
        pltpu.make_async_copy(ref, ref, semaphore).wait()

    def sources(chunk, j):
        if chunk == 0:
            for plane, ref in enumerate((key, key_other, value, value_other)):
                yield ref, pl.multiple_of(j * width, width), plane
        else:
            for place, ref in enumerate((query, query_other, cotangent)):
                for inner in range(per_chunk):
                    at = j * (group * width) + ((chunk - 1) * per_chunk + inner) * width
                    yield ref, pl.multiple_of(at, width), place * per_chunk + inner

    def first_of(chunk):
        return first_kv if chunk == 0 else first_q.at[chunk - 1]

    def start_first(chunk):
        at = pl.multiple_of(head * rows_here, 8)
        for some in range(4 if chunk == 0 else 1):

            def pieces(j):
                for ref, column, plane in sources(chunk, j):
                    if chunk or plane == some:
                        arrived = recv1_q.at[chunk - 1] if chunk else recv1_kv.at[plane]
                        target = first_of(chunk).at[plane, pl.ds(at, rows_here), :]
                        yield ref.at[:, pl.ds(column, width)], target, arrived

            def to(i, carry):
                j = (head + i) % heads
                for source, target, arrived in pieces(j):
                    remote(source, target, send1.at[chunk], arrived, (me, j)).start()
                return carry

            lax.fori_loop(1, heads, to, 0)
            for source, target, arrived in pieces(head):
                pltpu.make_async_copy(source, target, arrived).start()

    def spread(source, target, send, arrived):
        for i in range(1, SUB):
            to = (sub + i) % SUB
            remote(source(to), target, send, arrived, (z * SUB + to, head)).start()
        pltpu.make_async_copy(source(sub), target, arrived).start()

    start_first(0)

    segment = segments[...]
    lane = iota((1, width), 1)
    starts = jnp.zeros((1, width), F32)
    for g in range(1, PAIRS_PER_BIN):
        start = jnp.sum(jnp.where(segment < g, 1.0, 0.0), axis=1, keepdims=True)
        starts = jnp.where(lane == g, start, starts)
    starts_in[z] = jnp.broadcast_to(starts, (8, width))

    def tell(i, carry):
        remote(
            starts_in.at[z], starts_in.at[z], small_send.at[0], small_recv.at[0],
            (along(i) * SUB + sub, head),
        ).start()
        return carry

    lax.fori_loop(1, ring, tell, 0)

    off_row = offsets[...].astype(F32)
    plan_row = plan[...].astype(F32)
    square = (n, n)
    same = iota(square, 0) == iota(square, 1)
    lanes = iota(square, 1).astype(F32)
    off_column = jnp.sum(jnp.where(same, off_row, 0.0), axis=1, keepdims=True)
    plan_column = jnp.sum(jnp.where(same, plan_row, 0.0), axis=1, keepdims=True)
    distance = jnp.sum(jnp.where(plan_column == lanes, off_row, 0.0), axis=1, keepdims=True)
    target = me.astype(F32) + distance
    target = jnp.where(target >= n, target - n, target)
    wide = (n, rows)
    one = (1, rows)
    block = iota(wide, 1) // ROWS
    target_row = jnp.sum(jnp.where(iota(wide, 0) == block, target, 0.0), axis=0, keepdims=True)
    key_in = target_row * ROWS + (iota(one, 1) % ROWS).astype(F32)
    out = iota((rows, 1), 0)
    to_sub, inside = out // share, out % share
    kv_bin = inside // part_rows * bins + inside % bins
    kv_row = inside % part_rows // bins

    def ordering(bin_z, row):
        key_to = ((bin_z * SUB + to_sub) * ROWS + row).astype(F32)
        return jnp.where(key_to == key_in, 1.0, 0.0).astype(BF16)

    def moved(order, block):
        high, middle, low = split3(block)
        result = jnp.dot(order, high, preferred_element_type=F32)
        result += jnp.dot(order, middle, preferred_element_type=F32)
        return result + jnp.dot(order, low, preferred_element_type=F32)

    order_kv = ordering(kv_bin, kv_row)
    order_q = ordering(inside % ring, inside // ring)

    def second_kv(plane):
        wait_for(first_kv.at[plane], recv1_kv.at[plane])
        send_kv[plane] = moved(order_kv, first_kv[plane]).reshape(SUB, GROUPS, part_rows, width)
        at = pl.multiple_of(z * ring_rows + sub * part_rows, 8)
        target = ring_kv.at[:, plane, pl.ds(at, part_rows), :]
        spread(lambda to: send_kv.at[plane, to], target, send2.at[0], recv2_kv.at[plane])

    def second_q(c):
        wait_for(first_q.at[c], recv1_q.at[c])
        for plane in range(0, planes, 2):
            both = jnp.concatenate([first_q[c, plane], first_q[c, plane + 1]], axis=1)
            both = moved(order_q, both)
            send_q[c, plane] = both[:, :width]
            send_q[c, plane + 1] = both[:, width:]
        target = bin_q.at[c, :, pl.ds(pl.multiple_of(sub * share, 8), share), :]
        spread(
            lambda to: send_q.at[c, :, pl.ds(pl.multiple_of(to * share, 8), share), :],
            target, send2.at[c + 1], recv2_q.at[c],
        )

    def plane_of(plane, origin):
        return ring_kv.at[:, plane, pl.ds(pl.multiple_of(origin * ring_rows, 8), ring_rows), :]

    def piece(g, origin):
        return ring_kv.at[g, :, pl.ds(pl.multiple_of(origin * ring_rows, 8), ring_rows), :]

    def turn_of(way):
        return 1 - 2 * way

    def next_of(way):
        return (along(turn_of(way)) * SUB + sub, head)

    def send_own(plane):
        wait_for(plane_of(plane, z), recv2_kv.at[plane])
        for place in range(GROUPS if plane == 3 else 1):
            held = piece(place, z).at[3] if plane == 3 else plane_of(plane, z)
            for way in range(2):
                arrived = own_recv.at[way, plane + place]
                remote(held, held, own_send.at[way], arrived, next_of(way)).start()

    def receive_first():
        for way in range(2):
            for plane in range(3):
                wait_for(plane_of(plane, along(-turn_of(way))), own_recv.at[way, plane])

    def ring_step(g, step):
        for way in range(2):
            held = piece(g, along(-turn_of(way) * step))
            half = held.at[pl.ds(2 * way, 2)]
            if step == 1:
                wait_for(held.at[3], own_recv.at[way, 3 + g])
            else:
                wait_for(half if step == reach else held, ring_recv.at[way, g, step - 2])
            if step < reach:
                going = half if step == reach - 1 else held
                remote(
                    going, going, ring_send.at[way, g], ring_recv.at[way, g, step - 1], next_of(way)
                ).start()

    second_kv(0)
    second_kv(1)
    send_own(0)
    second_kv(2)
    send_own(1)
    second_kv(3)
    start_first(1)
    send_own(2)
    send_own(3)

    q_index = iota((SUB * ROWS, 1), 0)
    q_source = z * SUB + q_index // ROWS
    k_source = iota(one, 1) // ROWS

    def describe(at, carry):
        which = at * SUB + sub
        starts = starts_in[at]
        k_distance = ((which - k_source + n) % n).astype(F32)
        k_slot = jnp.sum(
            jnp.where(off_column == k_distance, iota(wide, 0).astype(F32), 0.0), axis=0, keepdims=True
        )
        k_place = k_slot * ROWS + (iota(one, 1) % ROWS).astype(F32)
        q_distance = ((which - q_source + n) % n).astype(F32)
        tall = (SUB * ROWS, n)
        q_slot = jnp.sum(
            jnp.where(off_row == q_distance, iota(tall, 1).astype(F32), 0.0), axis=1, keepdims=True
        )
        q_place = q_slot * ROWS + (q_index % ROWS).astype(F32)
        begin = jnp.zeros_like(q_place)
        k_segment = jnp.zeros_like(k_place)
        for g in range(1, PAIRS_PER_BIN):
            start = starts[:1, g : g + 1]
            begin = jnp.where(q_place >= start, start, begin)
            k_segment += jnp.where(k_place >= start, 1.0, 0.0)
        allowed = jnp.logical_and(k_place <= q_place, k_place >= begin)
        bias[at] = jnp.where(allowed, 0.0, -jnp.inf)
        members[at] = jnp.where(k_segment == iota((8, rows), 0).astype(F32), 1.0, 0.0)
        return carry

    scale = width**-0.5

    def softmax(scores, mask):
        scores = scores * scale + mask
        raised = jnp.exp(scores - jnp.max(scores, axis=1, keepdims=True))
        return raised * (1.0 / jnp.sum(raised, axis=1, keepdims=True))

    def work(at):
        g, inner_bin = at // bins, at % bins

        def keys(plane):
            return ring_kv[g, plane, pl.ds(inner_bin, rows, stride=bins), :]

        def queries(place):
            found = [
                bin_q[i // per_chunk, place * per_chunk + i % per_chunk, pl.ds(at, SUB * ROWS, stride=ring), :]
                for i in range(group)
            ]
            return jnp.concatenate(found, axis=0)

        key_terms = jnp.concatenate([right_terms(keys(0)), right_terms(keys(1))], axis=0)
        value_terms = jnp.concatenate([right_terms(keys(2)), right_terms(keys(3))], axis=0)
        both = jnp.concatenate([left_terms(queries(0)), left_terms(queries(1))], axis=0)
        scores = product(both, key_terms)
        grads = product(left_terms(queries(2)), value_terms)
        count = group * SUB * ROWS
        top, bottom = scores[:count], scores[count:]
        plain = top[:, :rows]
        mask = jnp.concatenate([bias[at]] * group, axis=0)
        weight = softmax(plain, mask)
        weight_other = softmax(bottom[:, rows:], mask)
        part = weight * grads[:, :rows]
        row_dot = jnp.sum(part, axis=1, keepdims=True)
        slope = (part - weight * row_dot) * scale
        head_term = weight_other * grads[:, rows:] - part
        query_term = slope * (bottom[:, :rows] - plain)
        kv_term = slope * (top[:, rows:] - plain) + (weight * grads[:, rows:] - part)
        by_head = (group, SUB * ROWS, rows)
        sums = jnp.concatenate(
            [
                jnp.sum(head_term.reshape(by_head), axis=1),
                jnp.sum(query_term.reshape(by_head), axis=1),
                jnp.sum(kv_term.reshape(-1, 8, rows), axis=0),
            ],
            axis=0,
        )
        found = jnp.zeros((2 * group + 8, width), F32)
        member = members[at]
        for g in range(PAIRS_PER_BIN):
            line = jnp.sum(sums * member[g : g + 1], axis=1, keepdims=True)
            found = jnp.where(lane == g, line, found)
        part_out[at] = found

        @pl.when(at != z)
        def _():
            remote(
                part_out.at[at], part_in.at[z], small_send.at[1], small_recv.at[1], (at * SUB + sub, head)
            ).start()

        @pl.when(at == z)
        def _():
            pltpu.make_async_copy(part_out.at[at], part_in.at[z], small_recv.at[1]).start()

    others = starts_in.at[pl.ds(0, ring - 1)]
    receive_first()
    for tau in range(1, reach):
        for g in range(GROUPS):
            if tau - SKEW * g > 0:
                ring_step(g, tau - SKEW * g)
        if tau == 1:
            start_first(2)
            start_first(3)
            start_first(4)
            wait_for(others, small_send.at[0])
            wait_for(others, small_recv.at[0])
            lax.fori_loop(0, ring, describe, 0)
        for c, when in enumerate(TASKS):
            if tau == when:
                second_q(c)
    for c in range(CHUNKS):
        wait_for(bin_q.at[c], recv2_q.at[c])
    done = [reach - 1 - SKEW * g for g in range(GROUPS)]
    for g in range(GROUPS):
        while done[g] < reach:
            for i in range(g, GROUPS if SKEW else g + 1):
                done[i] += 1
                if done[i] > 0:
                    ring_step(i, done[i])

        def one_bin(i, carry):
            work(g * bins + i)
            return carry

        lax.fori_loop(0, bins, one_bin, 0)

    for chunk in range(CHUNKS + 1):
        wait_for(first_of(chunk).at[:, pl.ds(0, (heads - 1) * rows_here), :], send1.at[chunk])
        wait_for(first_of(chunk).at[:, pl.ds(0, (SUB - 1) * share), :], send2.at[chunk])
    for g in range(GROUPS):
        for way in range(2):
            wait_for(ring_kv.at[g, pl.ds(0, 2), pl.ds(0, (2 * reach - 3) * ring_rows), :], ring_send.at[way, g])
    for way in range(2):
        wait_for(ring_kv.at[:, :, pl.ds(0, ring_rows), :], own_send.at[way])
    wait_for(part_out.at[pl.ds(0, ring - 1)], small_send.at[1])
    wait_for(part_in, small_recv.at[1])
    total = jnp.sum(part_in[...], axis=0)
    shape = (2 * group + 8, width)
    eye = iota(shape, 0) == iota(shape, 1)
    for g in range(PAIRS_PER_BIN):
        line = jnp.where(eye, total[:, g : g + 1], 0.0)
        out_ref[g : g + 1, :] = jnp.sum(line, axis=0, keepdims=True)
    keyed = jnp.sum(total[2 * group :], axis=0, keepdims=True)
    out_ref[PAIRS_PER_BIN:, :] = jnp.broadcast_to(keyed, (8 - PAIRS_PER_BIN, width))


def shards(n, heads, *arrays):
    segments, plan, offsets = arrays[7:]
    group = arrays[0].shape[1] // arrays[1].shape[1]
    planes = 3 * group // CHUNKS
    rows = ROWS * n
    ring = n // SUB
    hbm = pl.BlockSpec(memory_space=pltpu.HBM)
    vmem = pl.BlockSpec(memory_space=pltpu.VMEM)
    dma = pltpu.SemaphoreType.DMA
    packed = pl.pallas_call(
        functools.partial(kernel, n, heads, group),
        out_shape=jax.ShapeDtypeStruct((8, HEAD_SIZE), F32),
        in_specs=[hbm] * 7 + [vmem] * 3,
        out_specs=vmem,
        scratch_shapes=[
            pltpu.VMEM((4, rows, HEAD_SIZE), F32),
            pltpu.VMEM((CHUNKS, planes, rows, HEAD_SIZE), F32),
            pltpu.VMEM((4, SUB, GROUPS, rows // SUB // GROUPS, HEAD_SIZE), F32),
            pltpu.VMEM((CHUNKS, planes, rows, HEAD_SIZE), F32),
            pltpu.VMEM((GROUPS, 4, ring * rows // GROUPS, HEAD_SIZE), F32),
            pltpu.VMEM((CHUNKS, planes, rows, HEAD_SIZE), F32),
            pltpu.VMEM((ring, SUB * ROWS, rows), F32),
            pltpu.VMEM((ring, 8, rows), F32),
            pltpu.VMEM((ring, 8, HEAD_SIZE), F32),
            pltpu.VMEM((ring, 2 * group + 8, HEAD_SIZE), F32),
            pltpu.VMEM((ring, 2 * group + 8, HEAD_SIZE), F32),
            dma((CHUNKS + 1,)),
            dma((4,)),
            dma((CHUNKS,)),
            dma((CHUNKS + 1,)),
            dma((4,)),
            dma((CHUNKS,)),
            dma((2,)),
            dma((2, 3 + GROUPS)),
            dma((2, GROUPS)),
            dma((2, GROUPS, ring // 2 - 1)),
            dma((2,)),
            dma((2,)),
        ],
        compiler_params=pltpu.CompilerParams(
            collective_id=0, has_side_effects=True, vmem_limit_bytes=60 * 1024 * 1024
        ),
    )(*arrays[:7], segments, plan, offsets.reshape(1, -1))
    found = packed[:PAIRS_PER_BIN]
    keyed = packed[PAIRS_PER_BIN : PAIRS_PER_BIN + 1, :PAIRS_PER_BIN]
    return found[:, :group], found[:, group : 2 * group], keyed.reshape(-1, 1)


def solution(mesh):
    rows = P(("dp", "head"), None)
    return jax.shard_map(
        functools.partial(shards, mesh.shape["dp"], mesh.shape["head"]),
        mesh=mesh,
        in_specs=(rows,) * 7 + (P("dp", None), P("dp", None), P()),
        out_specs=(P("dp", "head"),) * 3,
        check_vma=False,
    )
```
